32 devices in a mesh: ta: 16 (over z, y, x), row: 2 (over core).
Axes of the slice: x: 2, y: 2, z: 4, core: 2. Of those that a mesh axis runs over, the one named last changes fastest.
Arguments:
- movie: bfloat16 [2, 128, 128, 512], P('row', 'ta'), may hold values from -384 to 384
- shifts: int32 [2, 128, 4, 2], P('row', 'ta'), may hold values from -8 to 8
- footprint: bfloat16 [2, 128, 8, 512], P('row', 'ta'), may hold values from 0.25 to 1
- support: int32 [2, 128, 8, 512], P('row', 'ta'), may hold values 0 or 1
- neuron_ids: int32 [2, 128, 8], P('row', 'ta'), may hold values from 0 to 255, as said below
- owner_order: int32 [256], replicated, may hold values from 0 to 255, each once
- start_traces: float32 [256, 128], P(('ta', 'row')), may hold values from 0 to 2
Outputs:
- tile_movie: bfloat16 [2, 128, 128, 512], P('row', 'ta')
- traces: float32 [256, 128], P(('ta', 'row'))
The draws below stay inside these ranges and needn't reach their ends.
Inputs may be any that keep to these rules, and one draw needn't show every extreme that they name: `neuron_ids`: the neurons named by one tile's slots are distinct. Slot 0 of tile t of slab s names neuron s * 128 + t, and every slot of that tile names a neuron within 12 of it, counted modulo 256. `owner_order`: A permutation of all neurons.
All inputs are finite; a program needn't handle non-finite values. No bound on the sum of `support` on one device may be relied on, other than what follows from the above.
Results may differ from the reference program's by a relative error of at most 0.004.
Values may be sent and summed in bfloat16 or wider, within the bound.
A program may use at most 64 MiB of HBM per device.

```python
import jax
import jax.numpy as jnp
from jax import lax

H = 128
W = 512
TH = 16
TW = 32
PW = 128
MAXS = 8
SLOTS = 8
REACH = 12
ITERS = 2
FRAMES = 128
SLABS = 2
PATCHES = 4
TILES = 128
TPIX = 512
NEURONS = 256


def draw_neuron_ids(key, part):
    tile_total = SLABS * TILES
    tile_keys = jax.random.split(jax.random.fold_in(key, 17), tile_total)

    def offsets(tile_key):
        order = jax.random.permutation(tile_key, 2 * REACH)
        picked = order[:SLOTS - 1].astype(jnp.int32)
        signed = jnp.where(picked < REACH, picked - REACH, picked - REACH + 1)
        return jnp.concatenate([jnp.zeros((1,), jnp.int32), signed])
    moves = jax.vmap(offsets)(tile_keys)
    home = jnp.arange(tile_total, dtype=jnp.int32) * (NEURONS // tile_total)
    return ((home[:, None] + moves) % NEURONS).reshape(SLABS, TILES, SLOTS).astype(jnp.int32)


def with_ends(entries, rng, least, high):
    longest = entries.shape.index(max(entries.shape))
    spots = []
    for shift in (0, 1):
        where = [jax.random.randint(jax.random.fold_in(rng, axis), (), 0, length) for axis, length in enumerate(entries.shape)]
        where[longest] = (where[longest] + shift) % entries.shape[longest]
        spots.append(tuple(where))
    return entries.at[spots[0]].set(least).at[spots[1]].set(high)


def levels(own_key, dims, pieces, least, high):
    def one(axis_at, blocks):
        steps = jax.random.uniform(jax.random.fold_in(jax.random.fold_in(own_key, 6), axis_at), (blocks,), jnp.float32, least / len(pieces), high / len(pieces))
        return jnp.repeat(jnp.exp(steps), dims[axis_at] // blocks).reshape((-1,) + (1,) * (len(dims) - axis_at - 1))

    gain = one(*pieces[0])
    for cut in pieces[1:]:
        gain = gain * one(*cut)
    return gain


def centred(own_key, dims, width, limit, cuts=(), kind=jnp.bfloat16):
    drawn = jax.random.normal(own_key, dims, jnp.float32) * width
    if len(cuts) > 0:
        drawn = levels(own_key, dims, cuts, -0.22, 0.18) * drawn
    return jnp.clip(drawn, min=-limit, max=limit).astype(kind)


def setup_inputs(seed: int = 0) -> dict:
    key_list = jax.random.split(jax.random.key(seed), 8)
    movie = centred(key_list[0], (SLABS, FRAMES, H, W), 64.0, 384.0, ((0, 2), (1, 16)))
    shifts = with_ends(jax.random.randint(key_list[1], (SLABS, FRAMES, PATCHES, 2), 0 - MAXS, MAXS + 1), jax.random.fold_in(key_list[1], 1), 0 - MAXS, MAXS).astype(jnp.int32)
    footprint = jnp.clip(0.25 + 0.75 * jax.random.uniform(key_list[2], (SLABS, TILES, SLOTS, TPIX), jnp.float32) ** levels(key_list[2], (SLABS, TILES, SLOTS, TPIX), ((0, 2), (1, 16)), -0.2, 0.2), 0.25, 1.0).astype(jnp.bfloat16)
    support = with_ends((jax.random.randint(key_list[3], (SLABS, TILES, SLOTS, TPIX), 0, 2) < 1).astype(jnp.int32), jax.random.fold_in(key_list[3], 1), 0, 1)
    neuron_ids = draw_neuron_ids(jax.random.fold_in(key_list[7], 71), 0)
    owner_order = jax.random.permutation(key_list[5], NEURONS).astype(jnp.int32)
    start_traces = jnp.clip(2.0 * jax.random.uniform(key_list[6], (NEURONS, FRAMES), jnp.float32) ** levels(key_list[6], (NEURONS, FRAMES), ((0, 32),), -0.2, 0.2), 0.0, 2.0)
    return dict(movie=movie, shifts=shifts, footprint=footprint, support=support, neuron_ids=neuron_ids, owner_order=owner_order, start_traces=start_traces)


def smoothing_table(length):
    places = jnp.arange(length, dtype=jnp.float32)
    spread = places[:, None] - places[None, :]
    kernel = jnp.exp(-spread * spread / 32.0)
    return (kernel / jnp.sum(kernel, axis=0, keepdims=True)).astype(jnp.bfloat16)


def register_frame(frame_image, frame_moves):
    padded = jnp.pad(frame_image, MAXS)
    strips = []
    for patch_index in range(PATCHES):
        row_anchor = (MAXS + frame_moves[patch_index, 0]).astype(jnp.int32)
        col_anchor = (MAXS + patch_index * PW + frame_moves[patch_index, 1]).astype(jnp.int32)
        strips.append(lax.dynamic_slice(padded, (row_anchor, col_anchor), (H, PW)))
    return jnp.concatenate(strips, axis=1)


def reference(movie, shifts, footprint, support, neuron_ids, owner_order, start_traces):
    table_wide = smoothing_table(W)
    table_tall = smoothing_table(H)

    def filter_frame(frame_pair):
        registered = register_frame(frame_pair[0], frame_pair[1])
        wide = jnp.dot(registered, table_wide, preferred_element_type=jnp.float32).astype(jnp.bfloat16)
        wide = lax.optimization_barrier(wide)
        smooth = jnp.dot(table_tall.T, wide, preferred_element_type=jnp.float32)
        return (registered.astype(jnp.float32) - smooth).astype(jnp.bfloat16)

    slab_tiles = []
    for slab_index in range(SLABS):
        filtered = lax.map(filter_frame, (movie[slab_index], shifts[slab_index]))
        tiled = filtered.reshape(FRAMES, H // TH, TH, W // TW, TW).transpose(1, 3, 0, 2, 4)
        slab_tiles.append(tiled.reshape(TILES, FRAMES, TPIX))
    tile_movie = jnp.stack(slab_tiles, axis=0)

    footprints = footprint * support.astype(jnp.bfloat16)
    flat_prints = footprints.reshape(SLABS * TILES, SLOTS, TPIX)
    flat_movie = tile_movie.reshape(SLABS * TILES, FRAMES, TPIX)

    def project_tile(tile_pair):
        return jnp.dot(tile_pair[0], tile_pair[1].T, preferred_element_type=jnp.float32)

    projected = lax.map(project_tile, (flat_prints, flat_movie))
    prints_wide = flat_prints.astype(jnp.float32)
    gram = jnp.einsum("tip,tjp->tij", prints_wide, prints_wide, precision=lax.Precision.HIGHEST)
    flat_ids = neuron_ids.reshape(SLABS * TILES, SLOTS).astype(jnp.int32)
    coupling = jnp.zeros((NEURONS, NEURONS), jnp.float32).at[flat_ids[:, :, None], flat_ids[:, None, :]].add(gram)
    drive = jnp.zeros((NEURONS, FRAMES), jnp.float32).at[flat_ids].add(projected)
    bound = 1.0 + jnp.sum(coupling, axis=1)
    current = start_traces[owner_order]
    for iteration in range(ITERS):
        gradient = jnp.dot(coupling, current, precision=lax.Precision.HIGHEST) - drive
        current = jnp.maximum(current - gradient / bound[:, None], 0.0)
    traces = jnp.zeros((NEURONS, FRAMES), jnp.float32).at[owner_order].set(current)
    return tile_movie, traces
```

```python
import functools

import jax
import jax.numpy as jnp
import numpy as np
from jax import lax
from jax.experimental import pallas as pl
from jax.experimental.pallas import tpu as pltpu
from jax.sharding import PartitionSpec as P

TH = 16
TW = 32
MAXS = 8
REACH = 12
ITERS = 2
LANES = 128
CHUNK = 2
MESH = pl.DeviceIdType.MESH
F32 = jnp.float32
BF16 = jnp.bfloat16


def smoothing_table(length):
    places = np.arange(length, dtype=np.float32)
    spread = places[:, None] - places[None, :]
    kernel = np.exp(-spread * spread / np.float32(32.0)).astype(np.float32)
    return kernel / np.sum(kernel, axis=0, keepdims=True)


def row_of(place, height):
    tall = height // TH
    group = LANES // TW
    inner = TH // group
    return place % tall * TH + place // tall % inner * group + place // (tall * inner)


def split(x):
    high = x.astype(BF16)
    return high, (x - high.astype(F32)).astype(BF16)


def mm(a, b, contract=(1, 0)):
    return lax.dot_general(
        a, b, (((contract[0],), (contract[1],)), ((), ())), preferred_element_type=F32
    )


def pick(onehot, x, contract=(1, 0)):
    high, low = split(x)
    return mm(onehot, high, contract) + mm(onehot, low, contract)


def mm3(a, b):
    ah, al = a
    bh, bl = split(b)
    return mm(ah, bh) + (mm(ah, bl) + mm(al, bh))


def filter_frame(frame, moves, wide_table, tall_table, stage, slot):
    height, breadth = frame.shape
    patches = len(moves)
    width = breadth // patches
    image = frame.astype(F32)
    lane = lax.broadcasted_iota(jnp.int32, (height, width), 1)
    place = lax.broadcasted_iota(jnp.int32, (height, height), 0)
    wanted = row_of(place, height)
    source = lax.broadcasted_iota(jnp.int32, (height, height), 1)
    strips = []
    for patch, (dy, dx) in enumerate(moves):
        blank = jnp.zeros((height, width), F32)
        here = image[:, patch * width : (patch + 1) * width]
        left = image[:, (patch - 1) * width : patch * width] if patch else blank
        right = image[:, (patch + 1) * width : (patch + 2) * width] if patch < patches - 1 else blank
        turn = lax.rem(width - dx, width)
        beside = jnp.where(lane < width // 2, right, left)
        at = lane + dx
        inside = (at >= 0) & (at < width)
        moved = jnp.where(inside, pltpu.roll(here, turn, 1), pltpu.roll(beside, turn, 1))
        chosen = (source == wanted + dy).astype(F32).astype(BF16)
        strips.append(mm(chosen, moved.astype(BF16)))
    registered = jnp.concatenate(strips, axis=1)
    wide = mm(registered.astype(BF16), wide_table).astype(BF16)
    smooth = mm(tall_table, wide)
    filtered = (registered - smooth).astype(BF16).astype(F32)
    group = LANES // TW
    part = height // group
    tall = height // TH
    stride = (breadth // TW) * CHUNK
    which = lax.broadcasted_iota(jnp.int32, (part, LANES), 1) // TW
    for q in range(breadth // LANES):
        cols = [filtered[b * part : (b + 1) * part, q * LANES : (q + 1) * LANES] for b in range(group)]
        for r in range(group):
            out = None
            for b in range(group):
                shift = (b - r) * TW % LANES
                turned = pltpu.roll(cols[b], shift, 1) if shift else cols[b]
                out = turned if out is None else jnp.where(which == b, turned, out)
            for a in range(TH // group):
                stage[a, pl.ds((q * group + r) * CHUNK + slot, tall, stride=stride), :] = out[a * tall : (a + 1) * tall]


def filter_kernel(moves, movie, wide_table, tall_table, out, stage):
    chunk = pl.program_id(0)
    for slot in range(CHUNK):
        frame = chunk * CHUNK + slot
        shifts = [(moves[frame, 2 * p], moves[frame, 2 * p + 1]) for p in range(moves.shape[1] // 2)]
        filter_frame(movie[slot], shifts, wide_table[...], tall_table[...], stage, slot)
    for a in range(stage.shape[0]):
        out[0, :, a * LANES : (a + 1) * LANES] = stage[a].astype(BF16)


def trace_kernel(
    sizes,
    send, prints, support, ids, order, start,
    tiles_out, traces_out,
    land, stage, full, bands, starts, drives, projected,
    a2a_send, a2a_recv, band_send, band_recv, start_send, start_recv, drive_send, drive_recv,
):
    n_ta, n_row = sizes
    n_dev = n_ta * n_row
    chunks, _, rows, pixels = send.shape
    tiles, frames, _ = tiles_out.shape
    window = drives.shape[1]
    neurons = order.shape[1]
    own = start.shape[0]
    slots = prints.shape[0] // tiles
    local_frames = chunks * CHUNK
    ta, row = lax.axis_index("ta"), lax.axis_index("row")
    home = row * n_ta + ta
    owner = ta * n_row + row

    def others(body):
        def step(k, carry):
            body(lax.rem(home + k, n_dev))
            return carry
        lax.fori_loop(1, n_dev, step, 0)

    def device(n):
        return (lax.rem(n, n_ta), n // n_ta)

    barrier = pltpu.get_barrier_semaphore()
    others(lambda n: pl.semaphore_signal(barrier, inc=1, device_id=device(n), device_id_type=MESH))

    masked = prints[...] * support[...].astype(F32).astype(BF16)
    total = tiles * slots
    gram = mm(masked, masked, (1, 1))
    tile_a = lax.broadcasted_iota(jnp.int32, (total, total), 0) // slots
    tile_b = lax.broadcasted_iota(jnp.int32, (total, total), 1) // slots
    gram = jnp.where(tile_a == tile_b, gram, 0.0)
    spot = lax.rem(ids[...] - (home * tiles - REACH) + 2 * neurons, neurons)
    selector = (lax.broadcasted_iota(jnp.int32, (window, total), 0) == spot).astype(F32).astype(BF16)
    left = pick(selector, gram)
    high, low = split(left)
    band = mm(high, selector, (1, 1)) + mm(low, selector, (1, 1))
    folds = window // 8
    bands[home] = jnp.concatenate(
        [band[8 * k : 8 * k + 8] for k in range(folds)]
        + ([jnp.zeros((8, LANES - folds * window), F32)] if folds * window < LANES else []),
        axis=1,
    )
    starts[owner] = start[...]

    pl.semaphore_wait(barrier, n_dev - 1)

    def post(c, step):
        def go(k, carry):
            dest = lax.rem(ta + k, n_ta)
            pltpu.make_async_remote_copy(
                src_ref=send.at[c, dest], dst_ref=land.at[c, ta],
                send_sem=a2a_send.at[c], recv_sem=a2a_recv.at[c],
                device_id=(dest, row), device_id_type=MESH,
            ).start()
            return carry
        lax.fori_loop(1, n_ta, go, 0)

    def spread(buffer, index, send_sem, recv_sem):
        others(lambda n: pltpu.make_async_remote_copy(
            src_ref=buffer.at[index], dst_ref=buffer.at[index],
            send_sem=send_sem, recv_sem=recv_sem,
            device_id=device(n), device_id_type=MESH,
        ).start())

    def drain(buffer, sem):
        part = buffer.at[pl.ds(0, n_dev - 1)]
        pltpu.make_async_copy(part, part, sem).wait()

    spread(bands, home, band_send, band_recv)
    spread(starts, owner, start_send, start_recv)
    for c in range(chunks):
        post(c, None)
        land[c, ta] = send[c, ta]

    drain(bands, band_recv)
    drain(starts, start_recv)
    spots = lax.broadcasted_iota(jnp.int32, (n_dev * window, neurons), 0)
    names = lax.broadcasted_iota(jnp.int32, (n_dev * window, neurons), 1)
    named = lax.rem(spots // window * tiles + lax.rem(spots, window) - REACH + neurons, neurons)
    places = (named == names).astype(F32).astype(BF16)
    expand_a = lax.broadcasted_iota(jnp.int32, (window, neurons), 0)
    expand_b = lax.broadcasted_iota(jnp.int32, (window, neurons), 1)
    everyone = bands[...]
    stacked = jnp.concatenate(
        [everyone[:, :, window * k : window * k + window] for k in range(folds)], axis=1
    ).reshape(n_dev * window, window)
    expand = ((expand_a - REACH + neurons) % neurons == expand_b).astype(F32).astype(BF16)
    wide = pick_right(stacked, expand).reshape(n_dev, window, neurons)
    wide = jnp.concatenate(
        [(pltpu.roll(wide[n], n * tiles % neurons, 1) if n * tiles % neurons else wide[n])[None] for n in range(n_dev)],
        axis=0,
    ).reshape(n_dev * window, neurons)
    coupling = pick(places, wide, (0, 0))
    bound = 1.0 + jnp.sum(coupling, axis=1, keepdims=True)
    inverse = 1.0 / bound
    owners = (lax.broadcasted_iota(jnp.int32, (neurons, neurons), 0) == order[...]).astype(F32).astype(BF16)
    mine = (
        lax.broadcasted_iota(jnp.int32, (own, neurons), 0) + owner * own == order[...]
    ).astype(F32).astype(BF16)
    current = pick(owners, starts[...].reshape(neurons, frames), (0, 0))
    parts = split(coupling)
    base = current - mm3(parts, current) * inverse

    for c in range(chunks):
        part = land.at[c, pl.ds(0, n_ta - 1)]
        pltpu.make_async_copy(part, part, a2a_recv.at[c]).wait()
        block = land[c].reshape(n_ta * rows, pixels)
        for a in range(pixels // LANES):
            stage[a] = block[:, a * LANES : (a + 1) * LANES].astype(F32)
        for tile in range(tiles):
            for f in range(CHUNK):
                full_rows = pl.ds(tile * frames + c * CHUNK + f, n_ta, stride=local_frames)
                from_rows = pl.ds(tile * CHUNK + f, n_ta, stride=tiles * CHUNK)
                for a in range(pixels // LANES):
                    full[a, full_rows, :] = stage[a, from_rows, :]
    for tile in range(tiles):
        block = jnp.concatenate(
            [full[a, tile * frames : (tile + 1) * frames] for a in range(pixels // LANES)], axis=1
        ).astype(BF16)
        tiles_out[tile] = block
        projected[tile * slots : (tile + 1) * slots] = mm(
            masked[tile * slots : (tile + 1) * slots], block, (1, 1)
        )
    drives[home] = pick(selector, projected[...]).astype(BF16)
    spread(drives, home, drive_send, drive_recv)
    drain(drives, drive_recv)
    drive = mm(places, drives[...].reshape(n_dev * window, frames), (0, 0))
    for iteration in range(ITERS):
        if iteration:
            base = current - mm3(parts, current) * inverse
        current = jnp.maximum(base + drive * inverse, 0.0)
    traces_out[...] = pick(mine, current)

    drain(bands, band_send)
    drain(starts, start_send)
    drain(drives, drive_send)
    for c in range(chunks):
        part = land.at[c, pl.ds(0, n_ta - 1)]
        pltpu.make_async_copy(part, part, a2a_send.at[c]).wait()


def pick_right(x, onehot):
    high, low = split(x)
    return mm(high, onehot) + mm(low, onehot)


def local(sizes, movie, shifts, footprint, support, neuron_ids, owner_order, start_traces):
    n_ta, n_row = sizes
    _, local_frames, height, breadth = movie.shape
    patches = shifts.shape[2]
    tile_total = (height // TH) * (breadth // TW)
    pixels = TH * TW
    tiles, slots = footprint.shape[1:3]
    neurons = owner_order.shape[0]
    own, frames = start_traces.shape
    chunks = local_frames // CHUNK
    order = np.asarray([row_of(k, height) for k in range(height)])
    tall = smoothing_table(height)[order][:, order].T
    vmem = pl.BlockSpec(memory_space=pltpu.VMEM)
    send = pl.pallas_call(
        filter_kernel,
        grid=(chunks,),
        out_shape=jax.ShapeDtypeStruct((chunks, tile_total * CHUNK, pixels), BF16),
        in_specs=[
            pl.BlockSpec(memory_space=pltpu.SMEM),
            pl.BlockSpec((CHUNK, height, breadth), lambda c: (c, 0, 0)),
            pl.BlockSpec((breadth, breadth), lambda c: (0, 0)),
            pl.BlockSpec((height, height), lambda c: (0, 0)),
        ],
        out_specs=pl.BlockSpec((1, tile_total * CHUNK, pixels), lambda c: (c, 0, 0)),
        scratch_shapes=[pltpu.VMEM((pixels // LANES, tile_total * CHUNK, LANES), F32)],
        compiler_params=pltpu.CompilerParams(vmem_limit_bytes=24 * 2**20),
        name="filter",
    )(
        shifts[0].reshape(local_frames, patches * 2),
        movie[0],
        jnp.asarray(smoothing_table(breadth).astype(jnp.bfloat16)),
        jnp.asarray(tall.astype(jnp.bfloat16)),
    )
    rows = tiles * CHUNK
    send = send.reshape(chunks, n_ta, rows, pixels)
    n_dev = n_ta * n_row
    window = -(-(tiles + 2 * REACH) // 8) * 8
    band_lanes = -(-(window // 8 * window) // LANES) * LANES
    dma = pltpu.SemaphoreType.DMA
    tile_movie, traces = pl.pallas_call(
        functools.partial(trace_kernel, sizes),
        out_shape=(
            jax.ShapeDtypeStruct((tiles, frames, pixels), BF16),
            jax.ShapeDtypeStruct((own, frames), F32),
        ),
        in_specs=[vmem] * 6,
        out_specs=(vmem, vmem),
        scratch_shapes=[
            pltpu.VMEM((chunks, n_ta, rows, pixels), BF16),
            pltpu.VMEM((pixels // LANES, n_ta * rows, LANES), F32),
            pltpu.VMEM((pixels // LANES, tiles * frames, LANES), F32),
            pltpu.VMEM((n_dev, 8, band_lanes), F32),
            pltpu.VMEM((n_dev, own, frames), F32),
            pltpu.VMEM((n_dev, window, frames), BF16),
            pltpu.VMEM((tiles * slots, frames), F32),
            dma((chunks,)), dma((chunks,)), dma, dma, dma, dma, dma, dma,
        ],
        compiler_params=pltpu.CompilerParams(
            collective_id=0, has_side_effects=True, vmem_limit_bytes=56 * 2**20
        ),
        name="traces",
    )(
        send,
        footprint.reshape(tiles * slots, pixels),
        support.reshape(tiles * slots, pixels),
        neuron_ids.reshape(1, tiles * slots),
        owner_order.reshape(1, neurons),
        start_traces,
    )
    return tile_movie[None], traces


def solution(mesh):
    sizes = (mesh.shape["ta"], mesh.shape["row"])
    return jax.shard_map(
        functools.partial(local, sizes),
        mesh=mesh,
        in_specs=(
            P("row", "ta", None, None),
            P("row", "ta", None, None),
            P("row", "ta", None, None),
            P("row", "ta", None, None),
            P("row", "ta", None),
            P(),
            P(("ta", "row"), None),
        ),
        out_specs=(P("row", "ta", None, None), P(("ta", "row"), None)),
        check_vma=False,
    )
```

```python
import functools

import jax
import jax.numpy as jnp
import numpy as np
from jax import lax
from jax.experimental import pallas as pl
from jax.experimental.pallas import tpu as pltpu
from jax.sharding import PartitionSpec as P

TH = 16
TW = 32
MAXS = 8
REACH = 12
ITERS = 2
LANES = 128
CHUNK = 2
MESH = pl.DeviceIdType.MESH
F32 = jnp.float32
BF16 = jnp.bfloat16


def smoothing_table(length):
    places = np.arange(length, dtype=np.float32)
    spread = places[:, None] - places[None, :]
    kernel = np.exp(-spread * spread / np.float32(32.0)).astype(np.float32)
    return kernel / np.sum(kernel, axis=0, keepdims=True)


def row_of(place, height):
    tall = height // TH
    group = LANES // TW
    inner = TH // group
    return place % tall * TH + place // tall % inner * group + place // (tall * inner)


def split(x):
    high = x.astype(BF16)
    return high, (x - high.astype(F32)).astype(BF16)


def mm(a, b, contract=(1, 0)):
    return lax.dot_general(
        a, b, (((contract[0],), (contract[1],)), ((), ())), preferred_element_type=F32
    )


def pick(onehot, x, contract=(1, 0)):
    high, low = split(x)
    return mm(onehot, high, contract) + mm(onehot, low, contract)


def mm3(a, b):
    ah, al = a
    bh, bl = split(b)
    return mm(ah, bh) + (mm(ah, bl) + mm(al, bh))


def filter_frame(frame, moves, wide_table, tall_table, stage, slot):
    height, breadth = frame.shape
    patches = len(moves)
    width = breadth // patches
    image = frame.astype(F32)
    lane = lax.broadcasted_iota(jnp.int32, (height, width), 1)
    place = lax.broadcasted_iota(jnp.int32, (height, height), 0)
    wanted = row_of(place, height)
    source = lax.broadcasted_iota(jnp.int32, (height, height), 1)
    strips = []
    for patch, (dy, dx) in enumerate(moves):
        blank = jnp.zeros((height, width), F32)
        here = image[:, patch * width : (patch + 1) * width]
        left = image[:, (patch - 1) * width : patch * width] if patch else blank
        right = image[:, (patch + 1) * width : (patch + 2) * width] if patch < patches - 1 else blank
        turn = lax.rem(width - dx, width)
        beside = jnp.where(lane < width // 2, right, left)
        at = lane + dx
        inside = (at >= 0) & (at < width)
        moved = jnp.where(inside, pltpu.roll(here, turn, 1), pltpu.roll(beside, turn, 1))
        chosen = (source == wanted + dy).astype(F32).astype(BF16)
        strips.append(mm(chosen, moved.astype(BF16)))
    registered = jnp.concatenate(strips, axis=1)
    wide = mm(registered.astype(BF16), wide_table).astype(BF16)
    smooth = mm(tall_table, wide)
    filtered = (registered - smooth).astype(BF16).astype(F32)
    group = LANES // TW
    part = height // group
    tall = height // TH
    stride = (breadth // TW) * CHUNK
    which = lax.broadcasted_iota(jnp.int32, (part, LANES), 1) // TW
    for q in range(breadth // LANES):
        cols = [filtered[b * part : (b + 1) * part, q * LANES : (q + 1) * LANES] for b in range(group)]
        for r in range(group):
            out = None
            for b in range(group):
                shift = (b - r) * TW % LANES
                turned = pltpu.roll(cols[b], shift, 1) if shift else cols[b]
                out = turned if out is None else jnp.where(which == b, turned, out)
            for a in range(TH // group):
                stage[a, pl.ds((q * group + r) * CHUNK + slot, tall, stride=stride), :] = out[a * tall : (a + 1) * tall]


def trace_kernel(
    sizes,
    moves, movie, wide_table, tall_table, prints, support, ids, order, start,
    tiles_out, traces_out,
    frames_in, send, land, stage, full, bands, starts, drives, projected,
    movie_sem, a2a_send, a2a_recv, band_send, band_recv, start_send, start_recv, drive_send, drive_recv,
):
    n_ta, n_row = sizes
    n_dev = n_ta * n_row
    chunks, _, rows, pixels = send.shape
    tiles, frames, _ = tiles_out.shape
    window = drives.shape[1]
    neurons = order.shape[1]
    own = start.shape[0]
    slots = prints.shape[0] // tiles
    local_frames = chunks * CHUNK
    ta, row = lax.axis_index("ta"), lax.axis_index("row")
    home = row * n_ta + ta
    owner = ta * n_row + row

    def others(body):
        def step(k, carry):
            body(lax.rem(home + k, n_dev))
            return carry
        lax.fori_loop(1, n_dev, step, 0)

    def device(n):
        return (lax.rem(n, n_ta), n // n_ta)

    def fetch(c):
        piece = pl.ds(c * CHUNK, CHUNK)
        return pltpu.make_async_copy(movie.at[piece], frames_in.at[piece], movie_sem.at[c])

    for c in range(chunks):
        fetch(c).start()
    barrier = pltpu.get_barrier_semaphore()
    others(lambda n: pl.semaphore_signal(barrier, inc=1, device_id=device(n), device_id_type=MESH))

    masked = prints[...] * support[...].astype(F32).astype(BF16)
    total = tiles * slots
    gram = mm(masked, masked, (1, 1))
    tile_a = lax.broadcasted_iota(jnp.int32, (total, total), 0) // slots
    tile_b = lax.broadcasted_iota(jnp.int32, (total, total), 1) // slots
    gram = jnp.where(tile_a == tile_b, gram, 0.0)
    spot = lax.rem(ids[...] - (home * tiles - REACH) + 2 * neurons, neurons)
    selector = (lax.broadcasted_iota(jnp.int32, (window, total), 0) == spot).astype(F32).astype(BF16)
    left = pick(selector, gram)
    high, low = split(left)
    band = mm(high, selector, (1, 1)) + mm(low, selector, (1, 1))
    folds = window // 8
    bands[home] = jnp.concatenate(
        [band[8 * k : 8 * k + 8] for k in range(folds)]
        + ([jnp.zeros((8, LANES - folds * window), F32)] if folds * window < LANES else []),
        axis=1,
    )
    starts[owner] = start[...]

    def post(c):
        def go(k, carry):
            dest = lax.rem(ta + k, n_ta)
            pltpu.make_async_remote_copy(
                src_ref=send.at[c, dest], dst_ref=land.at[c, ta],
                send_sem=a2a_send.at[c], recv_sem=a2a_recv.at[c],
                device_id=(dest, row), device_id_type=MESH,
            ).start()
            return carry
        lax.fori_loop(1, n_ta, go, 0)

    def spread(buffer, index, send_sem, recv_sem):
        others(lambda n: pltpu.make_async_remote_copy(
            src_ref=buffer.at[index], dst_ref=buffer.at[index],
            send_sem=send_sem, recv_sem=recv_sem,
            device_id=device(n), device_id_type=MESH,
        ).start())

    def drain(buffer, sem):
        part = buffer.at[pl.ds(0, n_dev - 1)]
        pltpu.make_async_copy(part, part, sem).wait()

    def produce(c, carry):
        fetch(c).wait()
        for slot in range(CHUNK):
            frame = c * CHUNK + slot
            shifts = [(moves[frame, 2 * p], moves[frame, 2 * p + 1]) for p in range(moves.shape[1] // 2)]
            filter_frame(frames_in[frame], shifts, wide_table[...], tall_table[...], stage, slot)
        for a in range(pixels // LANES):
            send[c, :, :, a * LANES : (a + 1) * LANES] = stage[a].astype(BF16).reshape(n_ta, rows, LANES)

        @pl.when(c == 0)
        def _():
            pl.semaphore_wait(barrier, n_dev - 1)

        post(c)
        land[c, ta] = send[c, ta]

        @pl.when(c == 0)
        def _():
            spread(bands, home, band_send, band_recv)
            spread(starts, owner, start_send, start_recv)
        return carry

    lax.fori_loop(0, chunks, produce, 0)

    drain(bands, band_recv)
    drain(starts, start_recv)
    spots = lax.broadcasted_iota(jnp.int32, (n_dev * window, neurons), 0)
    names = lax.broadcasted_iota(jnp.int32, (n_dev * window, neurons), 1)
    named = lax.rem(spots // window * tiles + lax.rem(spots, window) - REACH + neurons, neurons)
    places = (named == names).astype(F32).astype(BF16)
    expand_a = lax.broadcasted_iota(jnp.int32, (window, neurons), 0)
    expand_b = lax.broadcasted_iota(jnp.int32, (window, neurons), 1)
    everyone = bands[...]
    stacked = jnp.concatenate(
        [everyone[:, :, window * k : window * k + window] for k in range(folds)], axis=1
    ).reshape(n_dev * window, window)
    expand = ((expand_a - REACH + neurons) % neurons == expand_b).astype(F32).astype(BF16)
    wide = pick_right(stacked, expand).reshape(n_dev, window, neurons)
    wide = jnp.concatenate(
        [(pltpu.roll(wide[n], n * tiles % neurons, 1) if n * tiles % neurons else wide[n])[None] for n in range(n_dev)],
        axis=0,
    ).reshape(n_dev * window, neurons)
    coupling = pick(places, wide, (0, 0))
    bound = 1.0 + jnp.sum(coupling, axis=1, keepdims=True)
    inverse = 1.0 / bound
    owners = (lax.broadcasted_iota(jnp.int32, (neurons, neurons), 0) == order[...]).astype(F32).astype(BF16)
    mine = (
        lax.broadcasted_iota(jnp.int32, (own, neurons), 0) + owner * own == order[...]
    ).astype(F32).astype(BF16)
    current = pick(owners, starts[...].reshape(neurons, frames), (0, 0))
    parts = split(coupling)
    base = current - mm3(parts, current) * inverse

    for c in range(chunks):
        part = land.at[c, pl.ds(0, n_ta - 1)]
        pltpu.make_async_copy(part, part, a2a_recv.at[c]).wait()
        block = land[c].reshape(n_ta * rows, pixels)
        for a in range(pixels // LANES):
            stage[a] = block[:, a * LANES : (a + 1) * LANES].astype(F32)
        for tile in range(tiles):
            for f in range(CHUNK):
                full_rows = pl.ds(tile * frames + c * CHUNK + f, n_ta, stride=local_frames)
                from_rows = pl.ds(tile * CHUNK + f, n_ta, stride=tiles * CHUNK)
                for a in range(pixels // LANES):
                    full[a, full_rows, :] = stage[a, from_rows, :]
    for tile in range(tiles):
        block = jnp.concatenate(
            [full[a, tile * frames : (tile + 1) * frames] for a in range(pixels // LANES)], axis=1
        ).astype(BF16)
        tiles_out[tile] = block
        projected[tile * slots : (tile + 1) * slots] = mm(
            masked[tile * slots : (tile + 1) * slots], block, (1, 1)
        )
    drives[home] = pick(selector, projected[...]).astype(BF16)
    spread(drives, home, drive_send, drive_recv)
    drain(drives, drive_recv)
    drive = mm(places, drives[...].reshape(n_dev * window, frames), (0, 0))
    for iteration in range(ITERS):
        if iteration:
            base = current - mm3(parts, current) * inverse
        current = jnp.maximum(base + drive * inverse, 0.0)
    traces_out[...] = pick(mine, current)

    drain(bands, band_send)
    drain(starts, start_send)
    drain(drives, drive_send)
    for c in range(chunks):
        part = land.at[c, pl.ds(0, n_ta - 1)]
        pltpu.make_async_copy(part, part, a2a_send.at[c]).wait()


def pick_right(x, onehot):
    high, low = split(x)
    return mm(high, onehot) + mm(low, onehot)


def local(sizes, movie, shifts, footprint, support, neuron_ids, owner_order, start_traces):
    n_ta, n_row = sizes
    _, local_frames, height, breadth = movie.shape
    patches = shifts.shape[2]
    pixels = TH * TW
    tiles, slots = footprint.shape[1:3]
    neurons = owner_order.shape[0]
    own, frames = start_traces.shape
    chunks = local_frames // CHUNK
    order = np.asarray([row_of(k, height) for k in range(height)])
    tall = smoothing_table(height)[order][:, order].T
    vmem = pl.BlockSpec(memory_space=pltpu.VMEM)
    rows = tiles * CHUNK
    n_dev = n_ta * n_row
    window = -(-(tiles + 2 * REACH) // 8) * 8
    band_lanes = -(-(window // 8 * window) // LANES) * LANES
    dma = pltpu.SemaphoreType.DMA
    tile_movie, traces = pl.pallas_call(
        functools.partial(trace_kernel, sizes),
        out_shape=(
            jax.ShapeDtypeStruct((tiles, frames, pixels), BF16),
            jax.ShapeDtypeStruct((own, frames), F32),
        ),
        in_specs=[pl.BlockSpec(memory_space=pltpu.SMEM), pl.BlockSpec(memory_space=pl.ANY)] + [vmem] * 7,
        out_specs=(vmem, vmem),
        scratch_shapes=[
            pltpu.VMEM((local_frames, height, breadth), BF16),
            pltpu.VMEM((chunks, n_ta, rows, pixels), BF16),
            pltpu.VMEM((chunks, n_ta, rows, pixels), BF16),
            pltpu.VMEM((pixels // LANES, n_ta * rows, LANES), F32),
            pltpu.VMEM((pixels // LANES, tiles * frames, LANES), F32),
            pltpu.VMEM((n_dev, 8, band_lanes), F32),
            pltpu.VMEM((n_dev, own, frames), F32),
            pltpu.VMEM((n_dev, window, frames), BF16),
            pltpu.VMEM((tiles * slots, frames), F32),
            dma((chunks,)), dma((chunks,)), dma((chunks,)), dma, dma, dma, dma, dma, dma,
        ],
        compiler_params=pltpu.CompilerParams(
            collective_id=0, has_side_effects=True, vmem_limit_bytes=56 * 2**20
        ),
        name="traces",
    )(
        shifts[0].reshape(local_frames, patches * 2),
        movie[0],
        jnp.asarray(smoothing_table(breadth).astype(jnp.bfloat16)),
        jnp.asarray(tall.astype(jnp.bfloat16)),
        footprint.reshape(tiles * slots, pixels),
        support.reshape(tiles * slots, pixels),
        neuron_ids.reshape(1, tiles * slots),
        owner_order.reshape(1, neurons),
        start_traces,
    )
    return tile_movie[None], traces


def solution(mesh):
    sizes = (mesh.shape["ta"], mesh.shape["row"])
    return jax.shard_map(
        functools.partial(local, sizes),
        mesh=mesh,
        in_specs=(
            P("row", "ta", None, None),
            P("row", "ta", None, None),
            P("row", "ta", None, None),
            P("row", "ta", None, None),
            P("row", "ta", None),
            P(),
            P(("ta", "row"), None),
        ),
        out_specs=(P("row", "ta", None, None), P(("ta", "row"), None)),
        check_vma=False,
    )
```

```python
import functools

import jax
import jax.numpy as jnp
import numpy as np
from jax import lax
from jax.experimental import pallas as pl
from jax.experimental.pallas import tpu as pltpu
from jax.sharding import PartitionSpec as P

TH = 16
TW = 32
MAXS = 8
REACH = 12
ITERS = 2
LANES = 128
CHUNK = 2
MESH = pl.DeviceIdType.MESH
F32 = jnp.float32
BF16 = jnp.bfloat16


def smoothing_table(length):
    places = np.arange(length, dtype=np.float32)
    spread = places[:, None] - places[None, :]
    kernel = np.exp(-spread * spread / np.float32(32.0)).astype(np.float32)
    return kernel / np.sum(kernel, axis=0, keepdims=True)


def row_of(place, height):
    tall = height // TH
    group = LANES // TW
    inner = TH // group
    return place % tall * TH + place // tall % inner * group + place // (tall * inner)


def split(x):
    high = x.astype(BF16)
    return high, (x - high.astype(F32)).astype(BF16)


def mm(a, b, contract=(1, 0)):
    return lax.dot_general(
        a, b, (((contract[0],), (contract[1],)), ((), ())), preferred_element_type=F32
    )


def pick(onehot, x, contract=(1, 0)):
    high, low = split(x)
    return mm(onehot, high, contract) + mm(onehot, low, contract)


def mm3(a, b):
    ah, al = a
    bh, bl = split(b)
    return mm(ah, bh) + (mm(ah, bl) + mm(al, bh))


def filter_frame(frame, moves, wide_table, tall_table, stage, slot):
    height, breadth = frame.shape
    patches = len(moves)
    width = breadth // patches
    image = frame.astype(F32)
    lane = lax.broadcasted_iota(jnp.int32, (height, width), 1)
    place = lax.broadcasted_iota(jnp.int32, (height, height), 0)
    wanted = row_of(place, height)
    source = lax.broadcasted_iota(jnp.int32, (height, height), 1)
    strips = []
    for patch, (dy, dx) in enumerate(moves):
        blank = jnp.zeros((height, width), F32)
        here = image[:, patch * width : (patch + 1) * width]
        left = image[:, (patch - 1) * width : patch * width] if patch else blank
        right = image[:, (patch + 1) * width : (patch + 2) * width] if patch < patches - 1 else blank
        turn = lax.rem(width - dx, width)
        beside = jnp.where(lane < width // 2, right, left)
        at = lane + dx
        inside = (at >= 0) & (at < width)
        moved = jnp.where(inside, pltpu.roll(here, turn, 1), pltpu.roll(beside, turn, 1))
        chosen = (source == wanted + dy).astype(F32).astype(BF16)
        strips.append(mm(chosen, moved.astype(BF16)))
    registered = jnp.concatenate(strips, axis=1)
    wide = mm(registered.astype(BF16), wide_table).astype(BF16)
    smooth = mm(tall_table, wide)
    filtered = (registered - smooth).astype(BF16).astype(F32)
    group = LANES // TW
    part = height // group
    tall = height // TH
    stride = (breadth // TW) * CHUNK
    which = lax.broadcasted_iota(jnp.int32, (part, LANES), 1) // TW
    for q in range(breadth // LANES):
        cols = [filtered[b * part : (b + 1) * part, q * LANES : (q + 1) * LANES] for b in range(group)]
        for r in range(group):
            out = None
            for b in range(group):
                shift = (b - r) * TW % LANES
                turned = pltpu.roll(cols[b], shift, 1) if shift else cols[b]
                out = turned if out is None else jnp.where(which == b, turned, out)
            for a in range(TH // group):
                stage[a, pl.ds((q * group + r) * CHUNK + slot, tall, stride=stride), :] = out[a * tall : (a + 1) * tall]


def trace_kernel(
    sizes,
    moves, movie, wide_table, tall_table, prints, support, ids, order, start,
    tiles_out, traces_out,
    frames_in, send, land, stage, full, tiles_vmem, masked_ref, bands, starts, partial, inbox, drives, projected,
    movie_sem, tiles_sem, a2a_send, a2a_recv, gather_sems, inbox_send, inbox_recv,
):
    n_ta, n_row = sizes
    n_dev = n_ta * n_row
    chunks, _, rows, pixels = send.shape
    tiles, frames, _ = tiles_out.shape
    reach = inbox.shape[0] // 2
    window = -(-(tiles + 2 * REACH) // 8) * 8
    folds = window // 8
    neurons = order.shape[1]
    own = start.shape[0]
    slots = prints.shape[0] // tiles
    local_frames = chunks * CHUNK
    ta, row = lax.axis_index("ta"), lax.axis_index("row")
    home = row * n_ta + ta
    owner = ta * n_row + row

    def partner(k):
        if n_ta & (n_ta - 1):
            return lax.rem(ta + k, n_ta)
        return ta ^ (n_ta - k)

    def along(body):
        def step(k, carry):
            body(partner(k))
            return carry
        lax.fori_loop(1, n_ta, step, 0)

    def near(body):
        for e in range(2 * reach + 1):
            if e != reach:
                body(e, lax.rem(home + e - reach + n_dev, n_dev))

    def device(n):
        return (lax.rem(n, n_ta), n // n_ta)

    def fetch(c):
        piece = pl.ds(c * CHUNK, CHUNK)
        return pltpu.make_async_copy(movie.at[piece], frames_in.at[piece], movie_sem.at[c])

    for c in range(chunks):
        fetch(c).start()
    barrier = pltpu.get_barrier_semaphore()

    def greet(target):
        pl.semaphore_signal(barrier, inc=1, device_id=target, device_id_type=MESH)

    along(lambda other: greet((other, row)))
    for k in range(1, n_row):
        greet((ta, lax.rem(row + k, n_row)))
    near(lambda e, n: greet(device(n)))
    greeted = n_ta - 1 + n_row - 1 + 2 * reach

    def names(first, count):
        flat = jnp.concatenate([ids[t : t + 1] for t in range(tiles)], axis=1)
        spot = lax.rem(flat - first + 2 * neurons, neurons)
        total = tiles * slots
        return (lax.broadcasted_iota(jnp.int32, (count, total), 0) == spot).astype(F32).astype(BF16)

    def measure_tiles():
        masked = prints[...] * support[...].astype(F32).astype(BF16)
        masked_ref[...] = masked
        total = tiles * slots
        gram = mm(masked, masked, (1, 1))
        tile_a = lax.broadcasted_iota(jnp.int32, (total, total), 0) // slots
        tile_b = lax.broadcasted_iota(jnp.int32, (total, total), 1) // slots
        gram = jnp.where(tile_a == tile_b, gram, 0.0)
        selector = names(home * tiles - REACH, window)
        high, low = split(pick(selector, gram))
        band = mm(high, selector, (1, 1)) + mm(low, selector, (1, 1))
        bands[home] = jnp.concatenate(
            [band[8 * k : 8 * k + 8] for k in range(folds)]
            + ([jnp.zeros((8, LANES - folds * window), F32)] if folds * window < LANES else []),
            axis=1,
        )
        starts[home] = start[...]

    def post(c):
        along(lambda dest: pltpu.make_async_remote_copy(
            src_ref=send.at[c, dest], dst_ref=land.at[c, ta],
            send_sem=a2a_send.at[c], recv_sem=a2a_recv.at[c],
            device_id=(dest, row), device_id_type=MESH,
        ).start())

    def wait(part, sem):
        pltpu.make_async_copy(part, part, sem).wait()

    def gather(buffer, which):
        along(lambda other: pltpu.make_async_remote_copy(
            src_ref=buffer.at[home], dst_ref=buffer.at[home],
            send_sem=gather_sems.at[which, 0], recv_sem=gather_sems.at[which, 1],
            device_id=(other, row), device_id_type=MESH,
        ).start())

    def relay(buffer, which):
        wait(buffer.at[pl.ds(0, n_ta - 1)], gather_sems.at[which, 1])
        slab = buffer.at[pl.ds(row * n_ta, n_ta)]
        for k in range(1, n_row):
            pltpu.make_async_remote_copy(
                src_ref=slab, dst_ref=slab,
                send_sem=gather_sems.at[which, 2], recv_sem=gather_sems.at[which, 3],
                device_id=(ta, lax.rem(row + k, n_row)), device_id_type=MESH,
            ).start()

    def gathered(buffer, which):
        if n_row > 1:
            wait(buffer.at[pl.ds(0, n_ta * (n_row - 1))], gather_sems.at[which, 3])

    def sent(buffer, which):
        wait(buffer.at[pl.ds(0, n_ta - 1)], gather_sems.at[which, 0])
        if n_row > 1:
            wait(buffer.at[pl.ds(0, n_ta * (n_row - 1))], gather_sems.at[which, 2])

    def produce(c, carry):
        fetch(c).wait()
        for slot in range(CHUNK):
            frame = c * CHUNK + slot
            shifts = [(moves[p, 0, frame], moves[p, 1, frame]) for p in range(moves.shape[0])]
            filter_frame(frames_in[frame], shifts, wide_table[...], tall_table[...], stage, slot)
        for a in range(pixels // LANES):
            send[c, :, :, a * LANES : (a + 1) * LANES] = stage[a].astype(BF16).reshape(n_ta, rows, LANES)

        @pl.when(c == 0)
        def _():
            pl.semaphore_wait(barrier, greeted)

        post(c)
        land[c, ta] = send[c, ta]

        @pl.when(c == 0)
        def _():
            measure_tiles()
            gather(bands, 0)
            gather(starts, 1)
        return carry

    lax.fori_loop(0, chunks, produce, 0)

    relay(bands, 0)
    relay(starts, 1)
    gathered(bands, 0)
    gathered(starts, 1)
    spots = lax.broadcasted_iota(jnp.int32, (n_dev * window, neurons), 0)
    wanted = lax.broadcasted_iota(jnp.int32, (n_dev * window, neurons), 1)
    named = lax.rem(spots // window * tiles + lax.rem(spots, window) - REACH + neurons, neurons)
    places = (named == wanted).astype(F32).astype(BF16)
    expand_a = lax.broadcasted_iota(jnp.int32, (window, neurons), 0)
    expand_b = lax.broadcasted_iota(jnp.int32, (window, neurons), 1)
    everyone = bands[...]
    stacked = jnp.concatenate(
        [everyone[:, :, window * k : window * k + window] for k in range(folds)], axis=1
    ).reshape(n_dev * window, window)
    expand = ((expand_a - REACH + neurons) % neurons == expand_b).astype(F32).astype(BF16)
    wide = pick_right(stacked, expand).reshape(n_dev, window, neurons)
    wide = jnp.concatenate(
        [(pltpu.roll(wide[n], n * tiles % neurons, 1) if n * tiles % neurons else wide[n])[None] for n in range(n_dev)],
        axis=0,
    ).reshape(n_dev * window, neurons)
    coupling = pick(places, wide, (0, 0))
    bound = 1.0 + jnp.sum(coupling, axis=1, keepdims=True)
    inverse = 1.0 / bound
    keeper = order[...] // own
    spot = (keeper % n_row * n_ta + keeper // n_row) * own + order[...] % own
    owners = (lax.broadcasted_iota(jnp.int32, (neurons, neurons), 0) == spot).astype(F32).astype(BF16)
    mine = (
        lax.broadcasted_iota(jnp.int32, (own, neurons), 0) + owner * own == order[...]
    ).astype(F32).astype(BF16)
    current = pick(owners, starts[...].reshape(neurons, frames), (0, 0))
    parts = split(coupling)
    base = current - mm3(parts, current) * inverse

    for c in range(chunks):
        wait(land.at[c, pl.ds(0, n_ta - 1)], a2a_recv.at[c])
        block = land[c].reshape(n_ta * rows, pixels)
        for a in range(pixels // LANES):
            stage[a] = block[:, a * LANES : (a + 1) * LANES].astype(F32)
        for tile in range(tiles):
            for f in range(CHUNK):
                full_rows = pl.ds(tile * frames + c * CHUNK + f, n_ta, stride=local_frames)
                from_rows = pl.ds(tile * CHUNK + f, n_ta, stride=tiles * CHUNK)
                for a in range(pixels // LANES):
                    full[a, full_rows, :] = stage[a, from_rows, :]
    for tile in range(tiles):
        block = jnp.concatenate(
            [full[a, tile * frames : (tile + 1) * frames] for a in range(pixels // LANES)], axis=1
        ).astype(BF16)
        tiles_vmem[tile] = block
        projected[tile * slots : (tile + 1) * slots] = mm(
            masked_ref[tile * slots : (tile + 1) * slots], block, (1, 1)
        )
    whole = pltpu.make_async_copy(tiles_vmem, tiles_out, tiles_sem)
    terms = pick(names((home - reach) * tiles, (2 * reach + 1) * tiles), projected[...])
    partial[...] = terms.reshape(2 * reach + 1, tiles, frames)

    near(lambda e, n: pltpu.make_async_remote_copy(
        src_ref=partial.at[e], dst_ref=inbox.at[e],
        send_sem=inbox_send, recv_sem=inbox_recv,
        device_id=device(n), device_id_type=MESH,
    ).start())
    whole.start()
    wait(inbox.at[pl.ds(0, 2 * reach)], inbox_recv)
    mine_drive = partial[reach]
    for e in range(2 * reach + 1):
        if e != reach:
            mine_drive = mine_drive + inbox[e]
    drives[home] = mine_drive
    gather(drives, 2)
    relay(drives, 2)
    gathered(drives, 2)
    drive = drives[...].reshape(neurons, frames)
    for iteration in range(ITERS):
        if iteration:
            base = current - mm3(parts, current) * inverse
        current = jnp.maximum(base + drive * inverse, 0.0)
    traces_out[...] = pick(mine, current)

    for which, buffer in enumerate((bands, starts, drives)):
        sent(buffer, which)
    wait(inbox.at[pl.ds(0, 2 * reach)], inbox_send)
    for c in range(chunks):
        wait(land.at[c, pl.ds(0, n_ta - 1)], a2a_send.at[c])
    whole.wait()


def pick_right(x, onehot):
    high, low = split(x)
    return mm(high, onehot) + mm(low, onehot)


def local(sizes, movie, shifts, footprint, support, neuron_ids, owner_order, start_traces):
    n_ta, n_row = sizes
    _, local_frames, height, breadth = movie.shape
    pixels = TH * TW
    tiles, slots = footprint.shape[1:3]
    neurons = owner_order.shape[0]
    own, frames = start_traces.shape
    chunks = local_frames // CHUNK
    order = np.asarray([row_of(k, height) for k in range(height)])
    tall = smoothing_table(height)[order][:, order].T
    vmem = pl.BlockSpec(memory_space=pltpu.VMEM)
    rows = tiles * CHUNK
    n_dev = n_ta * n_row
    window = -(-(tiles + 2 * REACH) // 8) * 8
    reach = -(-REACH // tiles)
    band_lanes = -(-(window // 8 * window) // LANES) * LANES
    dma = pltpu.SemaphoreType.DMA
    tile_movie, traces = pl.pallas_call(
        functools.partial(trace_kernel, sizes),
        out_shape=(
            jax.ShapeDtypeStruct((tiles, frames, pixels), BF16),
            jax.ShapeDtypeStruct((own, frames), F32),
        ),
        in_specs=[pl.BlockSpec(memory_space=pltpu.SMEM), pl.BlockSpec(memory_space=pl.ANY)] + [vmem] * 7,
        out_specs=(pl.BlockSpec(memory_space=pl.ANY), vmem),
        scratch_shapes=[
            pltpu.VMEM((local_frames, height, breadth), BF16),
            pltpu.VMEM((chunks, n_ta, rows, pixels), BF16),
            pltpu.VMEM((chunks, n_ta, rows, pixels), BF16),
            pltpu.VMEM((pixels // LANES, n_ta * rows, LANES), F32),
            pltpu.VMEM((pixels // LANES, tiles * frames, LANES), F32),
            pltpu.VMEM((tiles, frames, pixels), BF16),
            pltpu.VMEM((tiles * slots, pixels), BF16),
            pltpu.VMEM((n_dev, 8, band_lanes), F32),
            pltpu.VMEM((n_dev, own, frames), F32),
            pltpu.VMEM((2 * reach + 1, tiles, frames), F32),
            pltpu.VMEM((2 * reach + 1, tiles, frames), F32),
            pltpu.VMEM((n_dev, tiles, frames), F32),
            pltpu.VMEM((tiles * slots, frames), F32),
            dma((chunks,)), dma, dma((chunks,)), dma((chunks,)), dma((3, 4)), dma, dma,
        ],
        compiler_params=pltpu.CompilerParams(
            collective_id=0, has_side_effects=True, vmem_limit_bytes=56 * 2**20
        ),
        name="traces",
    )(
        shifts[0].transpose(1, 2, 0),
        movie[0],
        jnp.asarray(smoothing_table(breadth).astype(jnp.bfloat16)),
        jnp.asarray(tall.astype(jnp.bfloat16)),
        footprint.reshape(tiles * slots, pixels),
        support.reshape(tiles * slots, pixels),
        neuron_ids[0],
        owner_order.reshape(1, neurons),
        start_traces,
    )
    return tile_movie[None], traces


def solution(mesh):
    sizes = (mesh.shape["ta"], mesh.shape["row"])
    return jax.shard_map(
        functools.partial(local, sizes),
        mesh=mesh,
        in_specs=(
            P("row", "ta", None, None),
            P("row", "ta", None, None),
            P("row", "ta", None, None),
            P("row", "ta", None, None),
            P("row", "ta", None),
            P(),
            P(("ta", "row"), None),
        ),
        out_specs=(P("row", "ta", None, None), P(("ta", "row"), None)),
        check_vma=False,
    )
```

```python
import functools

import jax
import jax.numpy as jnp
import numpy as np
from jax import lax
from jax.experimental import pallas as pl
from jax.experimental.pallas import tpu as pltpu
from jax.sharding import PartitionSpec as P

TH = 16
TW = 32
MAXS = 8
REACH = 12
ITERS = 2
LANES = 128
CHUNK = 2
MESH = pl.DeviceIdType.MESH
F32 = jnp.float32
BF16 = jnp.bfloat16


def smoothing_table(length):
    places = np.arange(length, dtype=np.float32)
    spread = places[:, None] - places[None, :]
    kernel = np.exp(-spread * spread / np.float32(32.0)).astype(np.float32)
    return kernel / np.sum(kernel, axis=0, keepdims=True)


def row_of(place, height):
    tall = height // TH
    group = LANES // TW
    inner = TH // group
    return place % tall * TH + place // tall % inner * group + place // (tall * inner)


def split(x):
    high = x.astype(BF16)
    return high, (x - high.astype(F32)).astype(BF16)


def mm(a, b, contract=(1, 0)):
    return lax.dot_general(
        a, b, (((contract[0],), (contract[1],)), ((), ())), preferred_element_type=F32
    )


def pick(onehot, x, contract=(1, 0)):
    high, low = split(x)
    return mm(onehot, high, contract) + mm(onehot, low, contract)


def mm3(a, b):
    ah, al = a
    bh, bl = split(b)
    return mm(ah, bh) + (mm(ah, bl) + mm(al, bh))


def filter_frame(frame, moves, wide_table, tall_table, stage, slot):
    height, breadth = frame.shape
    patches = len(moves)
    width = breadth // patches
    image = frame.astype(F32)
    lane = lax.broadcasted_iota(jnp.int32, (height, width), 1)
    place = lax.broadcasted_iota(jnp.int32, (height, height), 0)
    wanted = row_of(place, height)
    source = lax.broadcasted_iota(jnp.int32, (height, height), 1)
    strips = []
    for patch, (dy, dx) in enumerate(moves):
        blank = jnp.zeros((height, width), F32)
        here = image[:, patch * width : (patch + 1) * width]
        left = image[:, (patch - 1) * width : patch * width] if patch else blank
        right = image[:, (patch + 1) * width : (patch + 2) * width] if patch < patches - 1 else blank
        turn = lax.rem(width - dx, width)
        beside = jnp.where(lane < width // 2, right, left)
        at = lane + dx
        inside = (at >= 0) & (at < width)
        moved = jnp.where(inside, pltpu.roll(here, turn, 1), pltpu.roll(beside, turn, 1))
        chosen = (source == wanted + dy).astype(F32).astype(BF16)
        strips.append(mm(chosen, moved.astype(BF16)))
    registered = jnp.concatenate(strips, axis=1)
    wide = mm(registered.astype(BF16), wide_table).astype(BF16)
    smooth = mm(tall_table, wide)
    filtered = (registered - smooth).astype(BF16).astype(F32)
    group = LANES // TW
    part = height // group
    tall = height // TH
    stride = (breadth // TW) * CHUNK
    which = lax.broadcasted_iota(jnp.int32, (part, LANES), 1) // TW
    for q in range(breadth // LANES):
        cols = [filtered[b * part : (b + 1) * part, q * LANES : (q + 1) * LANES] for b in range(group)]
        for r in range(group):
            out = None
            for b in range(group):
                shift = (b - r) * TW % LANES
                turned = pltpu.roll(cols[b], shift, 1) if shift else cols[b]
                out = turned if out is None else jnp.where(which == b, turned, out)
            for a in range(TH // group):
                stage[a, pl.ds((q * group + r) * CHUNK + slot, tall, stride=stride), :] = out[a * tall : (a + 1) * tall]


def trace_kernel(
    sizes,
    moves, movie, wide_table, tall_table, prints, support, ids, order, start,
    tiles_out, traces_out,
    frames_in, send, land, stage, full, tiles_vmem, masked_ref, bands, starts, drives, projected,
    movie_sem, tiles_sem, a2a_send, a2a_recv, gather_sems,
):
    n_ta, n_row = sizes
    n_dev = n_ta * n_row
    chunks, _, rows, pixels = send.shape
    tiles, frames, _ = tiles_out.shape
    window = drives.shape[1]
    folds = window // 8
    neurons = order.shape[1]
    own = start.shape[0]
    slots = prints.shape[0] // tiles
    local_frames = chunks * CHUNK
    ta, row = lax.axis_index("ta"), lax.axis_index("row")
    home = row * n_ta + ta
    owner = ta * n_row + row

    def partner(k):
        if n_ta & (n_ta - 1):
            return lax.rem(ta + k, n_ta)
        return ta ^ (n_ta - k)

    def along(body):
        def step(k, carry):
            body(partner(k))
            return carry
        lax.fori_loop(1, n_ta, step, 0)

    def fetch(c):
        piece = pl.ds(c * CHUNK, CHUNK)
        return pltpu.make_async_copy(movie.at[piece], frames_in.at[piece], movie_sem.at[c])

    for c in range(chunks):
        fetch(c).start()
    barrier = pltpu.get_barrier_semaphore()

    def greet(target):
        pl.semaphore_signal(barrier, inc=1, device_id=target, device_id_type=MESH)

    along(lambda other: greet((other, row)))
    for k in range(1, n_row):
        greet((ta, lax.rem(row + k, n_row)))
    greeted = n_ta - 1 + n_row - 1

    def names(first, count):
        flat = jnp.concatenate([ids[t : t + 1] for t in range(tiles)], axis=1)
        spot = lax.rem(flat - first + 2 * neurons, neurons)
        total = tiles * slots
        return (lax.broadcasted_iota(jnp.int32, (count, total), 0) == spot).astype(F32).astype(BF16)

    def measure_tiles():
        masked = prints[...] * support[...].astype(F32).astype(BF16)
        masked_ref[...] = masked
        total = tiles * slots
        gram = mm(masked, masked, (1, 1))
        tile_a = lax.broadcasted_iota(jnp.int32, (total, total), 0) // slots
        tile_b = lax.broadcasted_iota(jnp.int32, (total, total), 1) // slots
        gram = jnp.where(tile_a == tile_b, gram, 0.0)
        selector = names(home * tiles - REACH, window)
        high, low = split(pick(selector, gram))
        band = mm(high, selector, (1, 1)) + mm(low, selector, (1, 1))
        bands[home] = jnp.concatenate(
            [band[8 * k : 8 * k + 8] for k in range(folds)]
            + ([jnp.zeros((8, LANES - folds * window), F32)] if folds * window < LANES else []),
            axis=1,
        )
        starts[home] = start[...]

    def post(c):
        along(lambda dest: pltpu.make_async_remote_copy(
            src_ref=send.at[c, dest], dst_ref=land.at[c, ta],
            send_sem=a2a_send.at[c], recv_sem=a2a_recv.at[c],
            device_id=(dest, row), device_id_type=MESH,
        ).start())

    def wait(part, sem):
        pltpu.make_async_copy(part, part, sem).wait()

    def gather(buffer, which):
        along(lambda other: pltpu.make_async_remote_copy(
            src_ref=buffer.at[home], dst_ref=buffer.at[home],
            send_sem=gather_sems.at[which, 0], recv_sem=gather_sems.at[which, 1],
            device_id=(other, row), device_id_type=MESH,
        ).start())

    def relay(buffer, which):
        wait(buffer.at[pl.ds(0, n_ta - 1)], gather_sems.at[which, 1])
        slab = buffer.at[pl.ds(row * n_ta, n_ta)]
        for k in range(1, n_row):
            pltpu.make_async_remote_copy(
                src_ref=slab, dst_ref=slab,
                send_sem=gather_sems.at[which, 2], recv_sem=gather_sems.at[which, 3],
                device_id=(ta, lax.rem(row + k, n_row)), device_id_type=MESH,
            ).start()

    def gathered(buffer, which):
        if n_row > 1:
            wait(buffer.at[pl.ds(0, n_ta * (n_row - 1))], gather_sems.at[which, 3])

    def sent(buffer, which):
        wait(buffer.at[pl.ds(0, n_ta - 1)], gather_sems.at[which, 0])
        if n_row > 1:
            wait(buffer.at[pl.ds(0, n_ta * (n_row - 1))], gather_sems.at[which, 2])

    def produce(c, carry):
        fetch(c).wait()
        for slot in range(CHUNK):
            frame = c * CHUNK + slot
            shifts = [(moves[p, 0, frame], moves[p, 1, frame]) for p in range(moves.shape[0])]
            filter_frame(frames_in[frame], shifts, wide_table[...], tall_table[...], stage, slot)
        for a in range(pixels // LANES):
            send[c, :, :, a * LANES : (a + 1) * LANES] = stage[a].astype(BF16).reshape(n_ta, rows, LANES)

        @pl.when(c == 0)
        def _():
            pl.semaphore_wait(barrier, greeted)

        post(c)
        land[c, ta] = send[c, ta]

        @pl.when(c == 0)
        def _():
            measure_tiles()
            gather(bands, 0)
            gather(starts, 1)
        return carry

    lax.fori_loop(0, chunks, produce, 0)

    relay(bands, 0)
    relay(starts, 1)
    gathered(bands, 0)
    gathered(starts, 1)
    spots = lax.broadcasted_iota(jnp.int32, (n_dev * window, neurons), 0)
    wanted = lax.broadcasted_iota(jnp.int32, (n_dev * window, neurons), 1)
    named = lax.rem(spots // window * tiles + lax.rem(spots, window) - REACH + neurons, neurons)
    places = (named == wanted).astype(F32).astype(BF16)
    expand_a = lax.broadcasted_iota(jnp.int32, (window, neurons), 0)
    expand_b = lax.broadcasted_iota(jnp.int32, (window, neurons), 1)
    everyone = bands[...]
    stacked = jnp.concatenate(
        [everyone[:, :, window * k : window * k + window] for k in range(folds)], axis=1
    ).reshape(n_dev * window, window)
    expand = ((expand_a - REACH + neurons) % neurons == expand_b).astype(F32).astype(BF16)
    wide = pick_right(stacked, expand).reshape(n_dev, window, neurons)
    wide = jnp.concatenate(
        [(pltpu.roll(wide[n], n * tiles % neurons, 1) if n * tiles % neurons else wide[n])[None] for n in range(n_dev)],
        axis=0,
    ).reshape(n_dev * window, neurons)
    coupling = pick(places, wide, (0, 0))
    bound = 1.0 + jnp.sum(coupling, axis=1, keepdims=True)
    inverse = 1.0 / bound
    keeper = order[...] // own
    spot = (keeper % n_row * n_ta + keeper // n_row) * own + order[...] % own
    owners = (lax.broadcasted_iota(jnp.int32, (neurons, neurons), 0) == spot).astype(F32).astype(BF16)
    mine = (
        lax.broadcasted_iota(jnp.int32, (own, neurons), 0) + owner * own == order[...]
    ).astype(F32).astype(BF16)
    current = pick(owners, starts[...].reshape(neurons, frames), (0, 0))
    parts = split(coupling)
    base = current - mm3(parts, current) * inverse

    for c in range(chunks):
        wait(land.at[c, pl.ds(0, n_ta - 1)], a2a_recv.at[c])
        block = land[c].reshape(n_ta * rows, pixels)
        for a in range(pixels // LANES):
            stage[a] = block[:, a * LANES : (a + 1) * LANES].astype(F32)
        for tile in range(tiles):
            for f in range(CHUNK):
                full_rows = pl.ds(tile * frames + c * CHUNK + f, n_ta, stride=local_frames)
                from_rows = pl.ds(tile * CHUNK + f, n_ta, stride=tiles * CHUNK)
                for a in range(pixels // LANES):
                    full[a, full_rows, :] = stage[a, from_rows, :]
    for tile in range(tiles):
        block = jnp.concatenate(
            [full[a, tile * frames : (tile + 1) * frames] for a in range(pixels // LANES)], axis=1
        ).astype(BF16)
        tiles_vmem[tile] = block
        projected[tile * slots : (tile + 1) * slots] = mm(
            masked_ref[tile * slots : (tile + 1) * slots], block, (1, 1)
        )
    whole = pltpu.make_async_copy(tiles_vmem, tiles_out, tiles_sem)
    drives[home] = pick(names(home * tiles - REACH, window), projected[...]).astype(BF16)
    gather(drives, 2)
    whole.start()
    relay(drives, 2)
    gathered(drives, 2)
    drive = mm(places, drives[...].reshape(n_dev * window, frames), (0, 0))
    for iteration in range(ITERS):
        if iteration:
            base = current - mm3(parts, current) * inverse
        current = jnp.maximum(base + drive * inverse, 0.0)
    traces_out[...] = pick(mine, current)

    for which, buffer in enumerate((bands, starts, drives)):
        sent(buffer, which)
    for c in range(chunks):
        wait(land.at[c, pl.ds(0, n_ta - 1)], a2a_send.at[c])
    whole.wait()


def finish_kernel(tiles_in, traces_in, tiles_out, traces_out):
    tiles_out[...] = tiles_in[...]
    traces_out[...] = traces_in[...]


def pick_right(x, onehot):
    high, low = split(x)
    return mm(high, onehot) + mm(low, onehot)


def local(sizes, movie, shifts, footprint, support, neuron_ids, owner_order, start_traces):
    n_ta, n_row = sizes
    _, local_frames, height, breadth = movie.shape
    pixels = TH * TW
    tiles, slots = footprint.shape[1:3]
    neurons = owner_order.shape[0]
    own, frames = start_traces.shape
    chunks = local_frames // CHUNK
    order = np.asarray([row_of(k, height) for k in range(height)])
    tall = smoothing_table(height)[order][:, order].T
    vmem = pl.BlockSpec(memory_space=pltpu.VMEM)
    rows = tiles * CHUNK
    n_dev = n_ta * n_row
    window = -(-(tiles + 2 * REACH) // 8) * 8
    band_lanes = -(-(window // 8 * window) // LANES) * LANES
    dma = pltpu.SemaphoreType.DMA
    tile_movie, traces = pl.pallas_call(
        functools.partial(trace_kernel, sizes),
        out_shape=(
            jax.ShapeDtypeStruct((tiles, frames, pixels), BF16),
            jax.ShapeDtypeStruct((own, frames), F32),
        ),
        in_specs=[pl.BlockSpec(memory_space=pltpu.SMEM), pl.BlockSpec(memory_space=pl.ANY)] + [vmem] * 7,
        out_specs=(pl.BlockSpec(memory_space=pl.ANY), vmem),
        scratch_shapes=[
            pltpu.VMEM((local_frames, height, breadth), BF16),
            pltpu.VMEM((chunks, n_ta, rows, pixels), BF16),
            pltpu.VMEM((chunks, n_ta, rows, pixels), BF16),
            pltpu.VMEM((pixels // LANES, n_ta * rows, LANES), F32),
            pltpu.VMEM((pixels // LANES, tiles * frames, LANES), F32),
            pltpu.VMEM((tiles, frames, pixels), BF16),
            pltpu.VMEM((tiles * slots, pixels), BF16),
            pltpu.VMEM((n_dev, 8, band_lanes), F32),
            pltpu.VMEM((n_dev, own, frames), F32),
            pltpu.VMEM((n_dev, window, frames), BF16),
            pltpu.VMEM((tiles * slots, frames), F32),
            dma((chunks,)), dma, dma((chunks,)), dma((chunks,)), dma((3, 4)),
        ],
        compiler_params=pltpu.CompilerParams(
            collective_id=0, has_side_effects=True, vmem_limit_bytes=56 * 2**20
        ),
        name="traces",
    )(
        shifts[0].transpose(1, 2, 0),
        movie[0],
        jnp.asarray(smoothing_table(breadth).astype(jnp.bfloat16)),
        jnp.asarray(tall.astype(jnp.bfloat16)),
        footprint.reshape(tiles * slots, pixels),
        support.reshape(tiles * slots, pixels),
        neuron_ids[0],
        owner_order.reshape(1, neurons),
        start_traces,
    )
    steps = 2
    specs = (
        pl.BlockSpec((tiles, frames // steps, pixels), lambda i: (0, i, 0)),
        pl.BlockSpec((own, frames), lambda i: (0, 0)),
    )
    tile_movie, traces = pl.pallas_call(
        finish_kernel,
        grid=(steps,),
        out_shape=(
            jax.ShapeDtypeStruct((tiles, frames, pixels), BF16),
            jax.ShapeDtypeStruct((own, frames), F32),
        ),
        in_specs=list(specs),
        out_specs=specs,
        name="finish",
    )(tile_movie, traces)
    return tile_movie[None], traces


def solution(mesh):
    sizes = (mesh.shape["ta"], mesh.shape["row"])
    return jax.shard_map(
        functools.partial(local, sizes),
        mesh=mesh,
        in_specs=(
            P("row", "ta", None, None),
            P("row", "ta", None, None),
            P("row", "ta", None, None),
            P("row", "ta", None, None),
            P("row", "ta", None),
            P(),
            P(("ta", "row"), None),
        ),
        out_specs=(P("row", "ta", None, None), P(("ta", "row"), None)),
        check_vma=False,
    )
```

```python
import functools

import jax
import jax.numpy as jnp
import numpy as np
from jax import lax
from jax.experimental import pallas as pl
from jax.experimental.pallas import tpu as pltpu
from jax.sharding import PartitionSpec as P

TH = 16
TW = 32
MAXS = 8
REACH = 12
ITERS = 2
LANES = 128
CHUNK = 2
MESH = pl.DeviceIdType.MESH
F32 = jnp.float32
BF16 = jnp.bfloat16


def smoothing_table(length):
    places = np.arange(length, dtype=np.float32)
    spread = places[:, None] - places[None, :]
    kernel = np.exp(-spread * spread / np.float32(32.0)).astype(np.float32)
    return kernel / np.sum(kernel, axis=0, keepdims=True)


def row_of(place, height):
    tall = height // TH
    group = LANES // TW
    inner = TH // group
    return place % tall * TH + place // tall % inner * group + place // (tall * inner)


def split(x):
    high = x.astype(BF16)
    return high, (x - high.astype(F32)).astype(BF16)


def mm(a, b, contract=(1, 0)):
    return lax.dot_general(
        a, b, (((contract[0],), (contract[1],)), ((), ())), preferred_element_type=F32
    )


def pick(onehot, x, contract=(1, 0)):
    high, low = split(x)
    return mm(onehot, high, contract) + mm(onehot, low, contract)


def mm3(a, b):
    ah, al = a
    bh, bl = split(b)
    return mm(ah, bh) + (mm(ah, bl) + mm(al, bh))


def filter_frame(frame, moves, wide_table, tall_table, stage, slot):
    height, breadth = frame.shape
    patches = len(moves)
    width = breadth // patches
    image = frame.astype(F32)
    lane = lax.broadcasted_iota(jnp.int32, (height, width), 1)
    place = lax.broadcasted_iota(jnp.int32, (height, height), 0)
    wanted = row_of(place, height)
    source = lax.broadcasted_iota(jnp.int32, (height, height), 1)
    strips = []
    for patch, (dy, dx) in enumerate(moves):
        blank = jnp.zeros((height, width), F32)
        here = image[:, patch * width : (patch + 1) * width]
        left = image[:, (patch - 1) * width : patch * width] if patch else blank
        right = image[:, (patch + 1) * width : (patch + 2) * width] if patch < patches - 1 else blank
        turn = lax.rem(width - dx, width)
        beside = jnp.where(lane < width // 2, right, left)
        at = lane + dx
        inside = (at >= 0) & (at < width)
        moved = jnp.where(inside, pltpu.roll(here, turn, 1), pltpu.roll(beside, turn, 1))
        chosen = (source == wanted + dy).astype(F32).astype(BF16)
        strips.append(mm(chosen, moved.astype(BF16)))
    registered = jnp.concatenate(strips, axis=1)
    wide = mm(registered.astype(BF16), wide_table).astype(BF16)
    smooth = mm(tall_table, wide)
    filtered = (registered - smooth).astype(BF16).astype(F32)
    group = LANES // TW
    part = height // group
    tall = height // TH
    stride = (breadth // TW) * CHUNK
    which = lax.broadcasted_iota(jnp.int32, (part, LANES), 1) // TW
    for q in range(breadth // LANES):
        cols = [filtered[b * part : (b + 1) * part, q * LANES : (q + 1) * LANES] for b in range(group)]
        for r in range(group):
            out = None
            for b in range(group):
                shift = (b - r) * TW % LANES
                turned = pltpu.roll(cols[b], shift, 1) if shift else cols[b]
                out = turned if out is None else jnp.where(which == b, turned, out)
            for a in range(TH // group):
                stage[a, pl.ds((q * group + r) * CHUNK + slot, tall, stride=stride), :] = out[a * tall : (a + 1) * tall]


def trace_kernel(
    sizes,
    moves, movie, wide_table, tall_table, prints, support, ids, order, start,
    tiles_out, traces_out,
    frames_in, send, land, stage, full, tiles_vmem, masked_ref, bands, starts, drives, projected,
    movie_sem, tiles_sem, a2a_send, a2a_recv, gather_sems,
):
    n_ta, n_row = sizes
    n_dev = n_ta * n_row
    chunks, _, rows, pixels = send.shape
    tiles, frames, _ = tiles_out.shape
    window = drives.shape[1]
    folds = window // 8
    neurons = order.shape[1]
    own = start.shape[0]
    slots = prints.shape[0] // tiles
    local_frames = chunks * CHUNK
    ta, row = lax.axis_index("ta"), lax.axis_index("row")
    home = row * n_ta + ta
    owner = ta * n_row + row

    def partner(k):
        if n_ta & (n_ta - 1):
            return lax.rem(ta + k, n_ta)
        return ta ^ (n_ta - k)

    def along(body):
        def step(k, carry):
            body(partner(k))
            return carry
        lax.fori_loop(1, n_ta, step, 0)

    def fetch(c):
        piece = pl.ds(c * CHUNK, CHUNK)
        return pltpu.make_async_copy(movie.at[piece], frames_in.at[piece], movie_sem.at[c])

    for c in range(chunks):
        fetch(c).start()
    barrier = pltpu.get_barrier_semaphore()

    def greet(target):
        pl.semaphore_signal(barrier, inc=1, device_id=target, device_id_type=MESH)

    along(lambda other: greet((other, row)))
    for k in range(1, n_row):
        greet((ta, lax.rem(row + k, n_row)))
    greeted = n_ta - 1 + n_row - 1

    def names(first, count):
        flat = jnp.concatenate([ids[t : t + 1] for t in range(tiles)], axis=1)
        spot = lax.rem(flat - first + 2 * neurons, neurons)
        total = tiles * slots
        return (lax.broadcasted_iota(jnp.int32, (count, total), 0) == spot).astype(F32).astype(BF16)

    def measure_tiles():
        masked = prints[...] * support[...].astype(F32).astype(BF16)
        masked_ref[...] = masked
        total = tiles * slots
        gram = mm(masked, masked, (1, 1))
        tile_a = lax.broadcasted_iota(jnp.int32, (total, total), 0) // slots
        tile_b = lax.broadcasted_iota(jnp.int32, (total, total), 1) // slots
        gram = jnp.where(tile_a == tile_b, gram, 0.0)
        selector = names(home * tiles - REACH, window)
        high, low = split(pick(selector, gram))
        band = mm(high, selector, (1, 1)) + mm(low, selector, (1, 1))
        bands[home] = jnp.concatenate(
            [band[8 * k : 8 * k + 8] for k in range(folds)]
            + ([jnp.zeros((8, LANES - folds * window), F32)] if folds * window < LANES else []),
            axis=1,
        )
        starts[home] = start[...]

    def post(c):
        along(lambda dest: pltpu.make_async_remote_copy(
            src_ref=send.at[c, dest], dst_ref=land.at[c, ta],
            send_sem=a2a_send.at[c], recv_sem=a2a_recv.at[c],
            device_id=(dest, row), device_id_type=MESH,
        ).start())

    def wait(part, sem):
        pltpu.make_async_copy(part, part, sem).wait()

    def gather(buffer, which):
        along(lambda other: pltpu.make_async_remote_copy(
            src_ref=buffer.at[home], dst_ref=buffer.at[home],
            send_sem=gather_sems.at[which, 0], recv_sem=gather_sems.at[which, 1],
            device_id=(other, row), device_id_type=MESH,
        ).start())

    def relay(buffer, which):
        wait(buffer.at[pl.ds(0, n_ta - 1)], gather_sems.at[which, 1])
        slab = buffer.at[pl.ds(row * n_ta, n_ta)]
        for k in range(1, n_row):
            pltpu.make_async_remote_copy(
                src_ref=slab, dst_ref=slab,
                send_sem=gather_sems.at[which, 2], recv_sem=gather_sems.at[which, 3],
                device_id=(ta, lax.rem(row + k, n_row)), device_id_type=MESH,
            ).start()

    def gathered(buffer, which):
        if n_row > 1:
            wait(buffer.at[pl.ds(0, n_ta * (n_row - 1))], gather_sems.at[which, 3])

    def sent(buffer, which):
        wait(buffer.at[pl.ds(0, n_ta - 1)], gather_sems.at[which, 0])
        if n_row > 1:
            wait(buffer.at[pl.ds(0, n_ta * (n_row - 1))], gather_sems.at[which, 2])

    def produce(c, carry):
        fetch(c).wait()
        for slot in range(CHUNK):
            frame = c * CHUNK + slot
            shifts = [(moves[p, 0, frame], moves[p, 1, frame]) for p in range(moves.shape[0])]
            filter_frame(frames_in[frame], shifts, wide_table[...], tall_table[...], stage, slot)
        for a in range(pixels // LANES):
            send[c, :, :, a * LANES : (a + 1) * LANES] = stage[a].astype(BF16).reshape(n_ta, rows, LANES)

        @pl.when(c == 0)
        def _():
            pl.semaphore_wait(barrier, greeted)

        post(c)
        land[c, ta] = send[c, ta]

        @pl.when(c == 0)
        def _():
            measure_tiles()
            gather(bands, 0)
            gather(starts, 1)
        return carry

    lax.fori_loop(0, chunks, produce, 0)

    relay(bands, 0)
    relay(starts, 1)
    gathered(bands, 0)
    gathered(starts, 1)
    spots = lax.broadcasted_iota(jnp.int32, (neurons, n_dev * window), 1)
    wanted = lax.broadcasted_iota(jnp.int32, (neurons, n_dev * window), 0)
    named = lax.rem(spots // window * tiles + lax.rem(spots, window) - REACH + neurons, neurons)
    places = (named == wanted).astype(F32).astype(BF16)
    expand_a = lax.broadcasted_iota(jnp.int32, (window, neurons), 0)
    expand_b = lax.broadcasted_iota(jnp.int32, (window, neurons), 1)
    everyone = bands[...]
    stacked = jnp.concatenate(
        [everyone[:, :, window * k : window * k + window] for k in range(folds)], axis=1
    ).reshape(n_dev * window, window)
    expand = ((expand_a - REACH + neurons) % neurons == expand_b).astype(F32).astype(BF16)
    wide = pick_right(stacked, expand).reshape(n_dev, window, neurons)
    wide = jnp.concatenate(
        [(pltpu.roll(wide[n], n * tiles % neurons, 1) if n * tiles % neurons else wide[n])[None] for n in range(n_dev)],
        axis=0,
    ).reshape(n_dev * window, neurons)
    coupling = pick(places, wide)
    bound = 1.0 + jnp.sum(coupling, axis=1, keepdims=True)
    inverse = 1.0 / bound
    keeper = order[...] // own
    spot = (keeper % n_row * n_ta + keeper // n_row) * own + order[...] % own
    owners = (lax.broadcasted_iota(jnp.int32, (neurons, neurons), 0) == spot).astype(F32).astype(BF16)
    mine = (
        lax.broadcasted_iota(jnp.int32, (own, neurons), 0) + owner * own == order[...]
    ).astype(F32).astype(BF16)
    current = pick(owners, starts[...].reshape(neurons, frames), (0, 0))
    parts = split(coupling)
    base = current - mm3(parts, current) * inverse

    for c in range(chunks):
        wait(land.at[c, pl.ds(0, n_ta - 1)], a2a_recv.at[c])
        block = land[c].reshape(n_ta * rows, pixels)
        for a in range(pixels // LANES):
            stage[a] = block[:, a * LANES : (a + 1) * LANES].astype(F32)
        for tile in range(tiles):
            for f in range(CHUNK):
                full_rows = pl.ds(tile * frames + c * CHUNK + f, n_ta, stride=local_frames)
                from_rows = pl.ds(tile * CHUNK + f, n_ta, stride=tiles * CHUNK)
                for a in range(pixels // LANES):
                    full[a, full_rows, :] = stage[a, from_rows, :]
    for tile in range(tiles):
        block = jnp.concatenate(
            [full[a, tile * frames : (tile + 1) * frames] for a in range(pixels // LANES)], axis=1
        ).astype(BF16)
        tiles_vmem[tile] = block
        projected[tile * slots : (tile + 1) * slots] = mm(
            masked_ref[tile * slots : (tile + 1) * slots], block, (1, 1)
        )
    whole = pltpu.make_async_copy(tiles_vmem, tiles_out, tiles_sem)
    drives[home] = pick(names(home * tiles - REACH, window), projected[...]).astype(BF16)
    gather(drives, 2)
    whole.start()
    relay(drives, 2)
    gathered(drives, 2)
    drive = mm(places, drives[...].reshape(n_dev * window, frames))
    for iteration in range(ITERS):
        if iteration:
            base = current - mm3(parts, current) * inverse
        current = jnp.maximum(base + drive * inverse, 0.0)
    traces_out[...] = pick(mine, current)

    for which, buffer in enumerate((bands, starts, drives)):
        sent(buffer, which)
    for c in range(chunks):
        wait(land.at[c, pl.ds(0, n_ta - 1)], a2a_send.at[c])
    whole.wait()


def finish_kernel(tiles_in, traces_in, tiles_out, traces_out):
    tiles_out[...] = tiles_in[...]
    traces_out[...] = traces_in[...]


def pick_right(x, onehot):
    high, low = split(x)
    return mm(high, onehot) + mm(low, onehot)


def local(sizes, movie, shifts, footprint, support, neuron_ids, owner_order, start_traces):
    n_ta, n_row = sizes
    _, local_frames, height, breadth = movie.shape
    pixels = TH * TW
    tiles, slots = footprint.shape[1:3]
    neurons = owner_order.shape[0]
    own, frames = start_traces.shape
    chunks = local_frames // CHUNK
    order = np.asarray([row_of(k, height) for k in range(height)])
    tall = smoothing_table(height)[order][:, order].T
    vmem = pl.BlockSpec(memory_space=pltpu.VMEM)
    rows = tiles * CHUNK
    n_dev = n_ta * n_row
    window = -(-(tiles + 2 * REACH) // 8) * 8
    band_lanes = -(-(window // 8 * window) // LANES) * LANES
    dma = pltpu.SemaphoreType.DMA
    tile_movie, traces = pl.pallas_call(
        functools.partial(trace_kernel, sizes),
        out_shape=(
            jax.ShapeDtypeStruct((tiles, frames, pixels), BF16),
            jax.ShapeDtypeStruct((own, frames), F32),
        ),
        in_specs=[pl.BlockSpec(memory_space=pltpu.SMEM), pl.BlockSpec(memory_space=pl.ANY)] + [vmem] * 7,
        out_specs=(pl.BlockSpec(memory_space=pl.ANY), vmem),
        scratch_shapes=[
            pltpu.VMEM((local_frames, height, breadth), BF16),
            pltpu.VMEM((chunks, n_ta, rows, pixels), BF16),
            pltpu.VMEM((chunks, n_ta, rows, pixels), BF16),
            pltpu.VMEM((pixels // LANES, n_ta * rows, LANES), F32),
            pltpu.VMEM((pixels // LANES, tiles * frames, LANES), F32),
            pltpu.VMEM((tiles, frames, pixels), BF16),
            pltpu.VMEM((tiles * slots, pixels), BF16),
            pltpu.VMEM((n_dev, 8, band_lanes), F32),
            pltpu.VMEM((n_dev, own, frames), F32),
            pltpu.VMEM((n_dev, window, frames), BF16),
            pltpu.VMEM((tiles * slots, frames), F32),
            dma((chunks,)), dma, dma((chunks,)), dma((chunks,)), dma((3, 4)),
        ],
        compiler_params=pltpu.CompilerParams(
            collective_id=0, has_side_effects=True, vmem_limit_bytes=56 * 2**20
        ),
        name="traces",
    )(
        shifts[0].transpose(1, 2, 0),
        movie[0],
        jnp.asarray(smoothing_table(breadth).astype(jnp.bfloat16)),
        jnp.asarray(tall.astype(jnp.bfloat16)),
        footprint.reshape(tiles * slots, pixels),
        support.reshape(tiles * slots, pixels),
        neuron_ids[0],
        owner_order.reshape(1, neurons),
        start_traces,
    )
    steps = 2
    specs = (
        pl.BlockSpec((tiles, frames // steps, pixels), lambda i: (0, i, 0)),
        pl.BlockSpec((own, frames), lambda i: (0, 0)),
    )
    tile_movie, traces = pl.pallas_call(
        finish_kernel,
        grid=(steps,),
        out_shape=(
            jax.ShapeDtypeStruct((tiles, frames, pixels), BF16),
            jax.ShapeDtypeStruct((own, frames), F32),
        ),
        in_specs=list(specs),
        out_specs=specs,
        name="finish",
    )(tile_movie, traces)
    return tile_movie[None], traces


def solution(mesh):
    sizes = (mesh.shape["ta"], mesh.shape["row"])
    return jax.shard_map(
        functools.partial(local, sizes),
        mesh=mesh,
        in_specs=(
            P("row", "ta", None, None),
            P("row", "ta", None, None),
            P("row", "ta", None, None),
            P("row", "ta", None, None),
            P("row", "ta", None),
            P(),
            P(("ta", "row"), None),
        ),
        out_specs=(P("row", "ta", None, None), P(("ta", "row"), None)),
        check_vma=False,
    )
```
